32 devices in a mesh: grp: 4 (over y, core), ex: 2 (over x), tp: 4 (over z).
Axes of the slice: x: 2, y: 2, z: 4, core: 2. Of those that a mesh axis runs over, the one named last changes fastest.
Arguments:
- residual: bfloat16 [128, 2, 6144], P(('grp', 'ex'), None, 'tp'), may hold values from -34 to 34
- query_new: bfloat16 [128, 2, 6144], P(('grp', 'ex'), None, 'tp'), may hold values from -5 to 5
- key_new: bfloat16 [128, 2, 1024], P(('grp', 'ex'), None, 'tp'), may hold values from -8 to 8
- value_new: bfloat16 [128, 2, 1024], P(('grp', 'ex'), None, 'tp'), may hold values from -12 to 12
- key_cache: bfloat16 [128, 8, 512, 128], P(('grp', 'ex'), 'tp'), may hold values from -5 to 5
- value_cache: bfloat16 [128, 8, 512, 128], P(('grp', 'ex'), 'tp'), may hold values from -12 to 12
- lengths: int32 [128], P(('grp', 'ex')), may hold values from 128 to 512, as said below
- norm_gain: bfloat16 [6144], P('tp'), may hold values from 0.099609375 to 1.8984375
- router: float32 [6144, 8], P('tp'), may hold values from -0.078125 to 0.078125
- routes: int32 [128, 2, 2], P(('grp', 'ex')), may hold values from 0 to 7, all different within a row; in each aligned block of 32 rows (0 to 31, 32 to 63, ..., all dimensions but the last counted through in order) at most 16 rows name the same one
- w_gate: bfloat16 [8, 6144, 8192], P('ex', None, ('grp', 'tp')), may hold values from -0.078125 to 0.078125
- w_up: bfloat16 [8, 6144, 8192], P('ex', None, ('grp', 'tp')), may hold values from -0.078125 to 0.078125
- w_down: bfloat16 [8, 8192, 6144], P('ex', ('grp', 'tp')), may hold values from -0.09375 to 0.09375
Outputs:
- attended: bfloat16 [128, 2, 6144], P(('grp', 'ex'), None, 'tp')
- expert_mix: bfloat16 [128, 2, 6144], P(('grp', 'ex'), None, 'tp')
The draws below stay inside these ranges and needn't reach their ends.
Inputs may be any that keep to these rules, and one draw needn't show every extreme that they name: `routes`: over the rows of one device (aligned blocks of 32 rows, environments then steps) no expert is named more than 16 times, and in some blocks one is named exactly 16 times; a row's two experts differ. `lengths`: some environment's cache is full.
All inputs are finite; a program needn't handle non-finite values.
Results may differ from the reference program's by a relative error of at most 0.023.
Values may be sent and summed in bfloat16 or wider, within the bound.
A program may use at most 192 MiB of HBM per device.

```python
import math
import jax
import jax.numpy as jnp
import numpy as np
from jax import lax

D = 6144
H = 48
KVH = 8
HD = 128
EXPERTS = 8
TOPK = 2
FF = 8192
CTX = 512
STEPS = 2
ENV_DEV = 16
ENVS = 128
CAP = 16


def draw_key_cache(key, part):
    noise_key = jax.random.fold_in(key, 11)
    drawn = jnp.clip(jax.random.normal(noise_key, (ENVS, KVH, CTX, HD), jnp.float32), -4.0, 4.0)
    return drawn.astype(jnp.bfloat16)


def draw_query_new(key, part):
    noise_key = jax.random.fold_in(key, 12)
    full_shape = (ENVS, STEPS, KVH, H // KVH, HD)
    drawn = jnp.clip(jax.random.normal(noise_key, full_shape, jnp.float32), -4.0, 4.0)
    return drawn.reshape(ENVS, STEPS, D).astype(jnp.bfloat16)


def draw_residual(key, part):
    row_key, column_key, noise_key = jax.random.split(jax.random.fold_in(key, 13), 3)
    row_scale = jnp.exp(jax.random.uniform(row_key, (ENVS, STEPS, 1), jnp.float32, 0.0, math.log(10.0)))
    column_scale = 10.0 ** (jnp.arange(D, dtype=jnp.float32) / D) * jnp.exp(jax.random.uniform(column_key, (D,), jnp.float32, -0.3, 0.3))
    drawn = jnp.clip(jax.random.normal(noise_key, (ENVS, STEPS, D), jnp.float32), -4.0, 4.0)
    return (0.05 * drawn * row_scale * column_scale).astype(jnp.bfloat16)


def draw_lengths(key, part):
    fill_key, pick_key = jax.random.split(jax.random.fold_in(key, 14))
    drawn = jax.random.randint(fill_key, (ENVS,), CTX // 4, CTX + 1)
    longest = jax.random.randint(pick_key, (), 0, ENVS)
    return jnp.where(jnp.arange(ENVS) == longest, CTX, drawn).astype(jnp.int32)


def strengthened(values, own_key, source, target, blocks, factor):
    owner, partner = [(jnp.arange(values.shape[dim]) // (values.shape[dim] // blocks)).reshape([-1 if axis == dim else 1 for axis in range(values.ndim)]) for dim in (source, target)]
    chosen = jax.random.permutation(own_key, blocks)[partner]
    strong = (owner == chosen) | (owner == (partner + blocks // 2) % blocks)
    return jnp.where(strong, factor * values, values)


def block_scale(stream_key, shape, cuts, smallest, high):
    factor_of = 1.0
    for position, parts in cuts:
        heights = jax.random.uniform(jax.random.fold_in(jax.random.fold_in(stream_key, 6), position), (parts,), jnp.float32, smallest / len(cuts), high / len(cuts))
        factor_of = factor_of * jnp.repeat(jnp.exp(heights), shape[position] // parts).reshape((-1,) + (1,) * (len(shape) - 1 - position))
    return factor_of


def deal_out(key, own, number, rows, amount, top, bound, skew):
    ranking = jax.random.permutation(key, amount)
    heavy_load, usual = shares(amount, rows * top, bound, skew, True), shares(amount, rows * top, bound, skew, False)
    places = jnp.arange(amount)

    def named(tallies, rotation):
        used = int((tallies > 0).sum())
        fixed = max(1, used // 4)
        moved = fixed + (places - fixed + rotation * (used - fixed)) % max(1, amount - fixed)
        return jnp.zeros((amount,), jnp.int32).at[ranking[jnp.where(places < fixed, places, moved)]].set(jnp.asarray(tallies, jnp.int32))

    tallies = jnp.where(number % 4 == 0, named(heavy_load, number // 4), named(usual, number - number // 4 - 1))
    mixed = jax.random.permutation(jax.random.fold_in(own, 3), amount)
    donor, taker = mixed[0:amount // 2 * 2:2], mixed[1:amount // 2 * 2:2]
    room = jnp.minimum(tallies[donor] - 1, bound - tallies[taker]) // 2
    room = jnp.where((donor == ranking[0]) | (taker == ranking[0]) | (tallies[taker] == 0), 0, jnp.maximum(room, 0))
    moved = jax.random.randint(jax.random.fold_in(own, 4), (amount // 2,), 0, 1 << 20) % (room + 1)
    tallies = tallies.at[donor].add(-moved).at[taker].add(moved)
    labels = jnp.searchsorted(jnp.cumsum(tallies), jnp.arange(rows * top), side="right").astype(jnp.int32)
    listing = labels.reshape(top, rows).T
    listing = listing[jax.random.permutation(jax.random.fold_in(own, 1), rows)]
    rotation = jax.random.randint(jax.random.fold_in(own, 2), (rows, 1), 0, top)
    return jnp.take_along_axis(listing, (jnp.arange(top)[None, :] + rotation) % top, axis=1)


def shares(count, total, bound, skew, full):
    portions = [(1 << 20) // math.isqrt(standing ** skew) + 1 for standing in range(1, count + 1)]
    largest = bound if full else min(bound, max(-(-total // count), total * portions[0] // sum(portions)))
    least = 1 if total - largest >= count - 1 else 0
    holding, rest = [largest] + [least] * (count - 1), total - largest - least * (count - 1)
    while rest > 0:
        movable = [i for i in range(1, count) if holding[i] < largest] or [i for i in range(1, count) if holding[i] < bound]
        whole, remaining = sum([portions[i] for i in movable]), rest
        for i in movable:
            more = min(bound - holding[i], max(1, remaining * portions[i] // whole), rest)
            holding[i] = holding[i] + more
            rest = rest - more
    return np.array(holding)


def bell_draw(key, dims, spread, most, cuts=(), kind=jnp.bfloat16):
    gain = block_scale(key, dims, cuts, -0.22, 0.18) if cuts else 1.0
    entries = jax.random.normal(key, dims, jnp.float32) * spread * gain
    return jnp.minimum(jnp.maximum(entries, -most), most).astype(kind)


def bell_draw_with(rng, shape, scale, most, pieces, heavy, held_as=jnp.bfloat16):
    values = scale * jax.random.normal(rng, shape, jnp.float32)
    if pieces:
        values = values * block_scale(rng, shape, pieces, -0.22, 0.18)
    return jnp.clip(strengthened(values, jax.random.fold_in(rng, 3), *heavy), -most, most).astype(held_as)


def setup_inputs(seed: int = 0) -> dict:
    arg_keys = jax.random.split(jax.random.key(seed), 14)
    residual = draw_residual(jax.random.fold_in(arg_keys[13], 71), 0)
    query_new = draw_query_new(jax.random.fold_in(arg_keys[13], 71), 0)
    key_new = bell_draw(arg_keys[2], (ENVS, STEPS, KVH * HD), 2.0, 8.0, ((0, 8), (2, 4)))
    value_new = bell_draw(arg_keys[3], (ENVS, STEPS, KVH * HD), 3.0, 12.0, ((0, 8), (2, 4)))
    key_cache = draw_key_cache(jax.random.fold_in(arg_keys[13], 71), 0)
    value_cache = bell_draw(arg_keys[5], (ENVS, KVH, CTX, HD), 3.0, 12.0, ((0, 8), (1, 4)))
    lengths = draw_lengths(jax.random.fold_in(arg_keys[13], 71), 0)
    norm_gain = jnp.clip(1.0 + 0.18 * jax.random.normal(arg_keys[7], (D,), jnp.float32), 0.099609375, 1.8984375).astype(jnp.bfloat16)
    router = bell_draw(arg_keys[8], (D, EXPERTS), D ** -0.5, 0.078125, ((0, 4),), jnp.float32)
    routes_keys = jax.random.split(jax.random.fold_in(arg_keys[9], 1), ENVS * STEPS // (ENV_DEV * STEPS))
    routes_turns = jax.random.permutation(jax.random.fold_in(arg_keys[9], 3), ENVS * STEPS // (ENV_DEV * STEPS))
    routes = jax.vmap(lambda own, number: deal_out(jax.random.fold_in(arg_keys[9], 2), own, number, ENV_DEV * STEPS, EXPERTS, TOPK, CAP, 2))(routes_keys, routes_turns).reshape((ENVS, STEPS, TOPK))
    w_gate = bell_draw(arg_keys[10], (EXPERTS, D, FF), D ** -0.5, 0.078125, ((0, 2), (2, 16)))
    w_up = bell_draw(arg_keys[11], (EXPERTS, D, FF), D ** -0.5, 0.078125, ((0, 2), (2, 16)))
    w_down = bell_draw_with(arg_keys[12], (EXPERTS, FF, D), FF ** -0.5, 0.09375, ((0, 2), (1, 16)), (1, 2, 16, 2.0))
    return {"residual": residual, "query_new": query_new, "key_new": key_new, "value_new": value_new, "key_cache": key_cache, "value_cache": value_cache, "lengths": lengths, "norm_gain": norm_gain, "router": router, "routes": routes, "w_gate": w_gate, "w_up": w_up, "w_down": w_down}


def attend(query_new, key_new, value_new, key_cache, value_cache, lengths):
    env_count, step_count, feature_count = query_new.shape
    kv_count = key_cache.shape[1]
    context = key_cache.shape[2]
    head_dim = key_cache.shape[3]
    group_size = feature_count // (kv_count * head_dim)
    queries = query_new.astype(jnp.float32).reshape(env_count, step_count, kv_count, group_size, head_dim)
    keys_now = key_new.astype(jnp.float32).reshape(env_count, step_count, kv_count, head_dim)
    values_now = value_new.astype(jnp.float32).reshape(env_count, step_count, kv_count, head_dim)
    score_scale = head_dim ** (-0.5)
    cached = jnp.einsum('eskgd,ekcd->eskgc', queries, key_cache.astype(jnp.float32)) * score_scale
    fresh_scores = jnp.einsum('eskgd,etkd->eskgt', queries, keys_now) * score_scale
    valid_mask = (lax.broadcasted_iota(jnp.int32, (env_count, context), 1) < lengths[:, None].astype(jnp.int32))[:, None, None, None, :]
    causal = (lax.broadcasted_iota(jnp.int32, (step_count, step_count), 1) <= lax.broadcasted_iota(jnp.int32, (step_count, step_count), 0))[None, :, None, None, :]
    cached = jnp.where(valid_mask, cached, -1e+30)
    fresh_scores = jnp.where(causal, fresh_scores, -1e+30)
    row_top = jnp.maximum(lax.optimization_barrier(jnp.max(cached, -1)), lax.optimization_barrier(jnp.max(fresh_scores, -1)))[..., None]
    weight_cached = jnp.where(valid_mask, jnp.exp(cached - row_top), 0.0)
    weight_fresh = jnp.where(causal, jnp.exp(fresh_scores - row_top), 0.0)
    row_total = (lax.optimization_barrier(jnp.sum(weight_cached, -1)) + lax.optimization_barrier(jnp.sum(weight_fresh, -1)))[..., None]
    probs_cached = (weight_cached / row_total).astype(jnp.bfloat16).astype(jnp.float32)
    probs_fresh = (weight_fresh / row_total).astype(jnp.bfloat16).astype(jnp.float32)
    heads_out = jnp.einsum('eskgc,ekcd->eskgd', probs_cached, value_cache.astype(jnp.float32))
    heads_out = heads_out + jnp.einsum('eskgt,etkd->eskgd', probs_fresh, values_now)
    return heads_out.reshape(env_count, step_count, feature_count)

def reference(residual, query_new, key_new, value_new, key_cache, value_cache, lengths, norm_gain, router, routes, w_gate, w_up, w_down):
    state = residual.astype(jnp.float32) + attend(query_new, key_new, value_new, key_cache, value_cache, lengths)
    attended = state.astype(jnp.bfloat16)
    squares = lax.optimization_barrier(jnp.sum(state * state, -1))
    root_mean = jnp.sqrt(squares / D + 1e-05)[..., None]
    scaled = state * norm_gain.astype(jnp.float32)
    logits = jnp.einsum('esd,dx->esx', scaled, router, precision=lax.Precision.HIGHEST) / root_mean
    normed = (scaled / root_mean).astype(jnp.bfloat16)
    expert_ids = jnp.arange(EXPERTS, dtype=jnp.int32)
    picked_logits = lax.optimization_barrier(jnp.sum(jnp.where(routes[..., None] == expert_ids, logits[:, :, None, :], 0.0), -1))
    first_gate = 1.0 / (1.0 + jnp.exp(picked_logits[..., 1] - picked_logits[..., 0]))
    second_gate = 1.0 - first_gate
    flat_rows = normed.reshape(ENVS * STEPS, D)

    def expert_rows(expert_id):
        gate_part = jnp.dot(flat_rows, w_gate[expert_id], preferred_element_type=jnp.float32)
        up_part = jnp.dot(flat_rows, w_up[expert_id], preferred_element_type=jnp.float32)
        hidden = (jax.nn.silu(gate_part) * up_part).astype(jnp.bfloat16)
        return jnp.dot(hidden, w_down[expert_id], preferred_element_type=jnp.float32).astype(jnp.bfloat16)
    outputs = lax.map(expert_rows, expert_ids)
    chosen = (routes.reshape(ENVS * STEPS, TOPK)[:, :, None] == expert_ids[None, None, :]).astype(jnp.float32)
    picked_rows = jnp.einsum('rkx,xrd->rkd', chosen, outputs.astype(jnp.float32), precision=lax.Precision.HIGHEST)
    picked_rows = picked_rows.reshape(ENVS, STEPS, TOPK, D)
    expert_mix = first_gate[..., None] * picked_rows[:, :, 0] + second_gate[..., None] * picked_rows[:, :, 1]
    return (attended, expert_mix.astype(jnp.bfloat16))
```

```python
import functools

import jax
import jax.numpy as jnp
from jax import lax
from jax.experimental import pallas as pl
from jax.experimental.pallas import tpu as pltpu
from jax.sharding import PartitionSpec as P

LANES = 128


def attend(query_new, key_new, value_new, key_cache, value_cache, lengths):
    env_count, step_count, feature_count = query_new.shape
    kv_count = key_cache.shape[1]
    context = key_cache.shape[2]
    head_dim = key_cache.shape[3]
    group_size = feature_count // (kv_count * head_dim)
    queries = query_new.reshape(env_count, step_count, kv_count, group_size, head_dim)
    keys_now = key_new.reshape(env_count, step_count, kv_count, head_dim)
    values_now = value_new.reshape(env_count, step_count, kv_count, head_dim)
    score_scale = head_dim ** (-0.5)
    cached = (
        jnp.einsum("eskgd,ekcd->eskgc", queries, key_cache, preferred_element_type=jnp.float32)
        * score_scale
    )
    fresh_scores = (
        jnp.einsum("eskgd,etkd->eskgt", queries, keys_now, preferred_element_type=jnp.float32)
        * score_scale
    )
    valid_mask = (lax.broadcasted_iota(jnp.int32, (env_count, context), 1) < lengths[:, None])[
        :, None, None, None, :
    ]
    causal = (
        lax.broadcasted_iota(jnp.int32, (step_count, step_count), 1)
        <= lax.broadcasted_iota(jnp.int32, (step_count, step_count), 0)
    )[None, :, None, None, :]
    cached = jnp.where(valid_mask, cached, -1e30)
    fresh_scores = jnp.where(causal, fresh_scores, -1e30)
    row_top = jnp.maximum(jnp.max(cached, -1), jnp.max(fresh_scores, -1))[..., None]
    weight_cached = jnp.where(valid_mask, jnp.exp(cached - row_top), 0.0)
    weight_fresh = jnp.where(causal, jnp.exp(fresh_scores - row_top), 0.0)
    row_total = (jnp.sum(weight_cached, -1) + jnp.sum(weight_fresh, -1))[..., None]
    probs_cached = (weight_cached / row_total).astype(jnp.bfloat16)
    probs_fresh = (weight_fresh / row_total).astype(jnp.bfloat16)
    heads_out = jnp.einsum(
        "eskgc,ekcd->eskgd", probs_cached, value_cache, preferred_element_type=jnp.float32
    )
    heads_out = heads_out + jnp.einsum(
        "eskgt,etkd->eskgd", probs_fresh, values_now, preferred_element_type=jnp.float32
    )
    return heads_out.reshape(env_count, step_count, feature_count)


def expert_kernel(
    shards, experts_here, width, slice_width, got, gate_w, up_w, down_w, out, gate_acc, up_acc, hidden, inverse, gates
):
    step = pl.program_id(0)
    sources, _, rows, _ = got.shape
    tokens = sources * rows
    shard = lax.rem(step, shards)
    expert = lax.div(step, shards)
    first_phase = experts_here * shards

    @pl.when(step == 0)
    def _():
        info = jnp.zeros((tokens, LANES), jnp.float32)
        for k in range(shards):
            info += got[:, k, :, slice_width:].astype(jnp.float32).reshape(tokens, LANES)
        routed = got[:, 0, :, slice_width:].astype(jnp.float32).reshape(tokens, LANES)
        squares = info[:, 0:1] + info[:, 1:2] + info[:, 2:3]
        root_mean = jnp.sqrt(squares / width + 1e-05)
        difference = (info[:, 3:4] + info[:, 4:5] + info[:, 5:6]) / root_mean
        first = 1.0 / (1.0 + jnp.exp(difference))
        inverse[...] = 1.0 / root_mean
        base = lax.axis_index("ex") * experts_here
        for e in range(experts_here):
            own = (base + e).astype(jnp.float32)
            gates[e] = jnp.where(routed[:, 6:7] == own, first, 0.0) + jnp.where(
                routed[:, 7:8] == own, 1.0 - first, 0.0
            )

    @pl.when(step < first_phase)
    def _():
        block = got[:, shard, :, :slice_width].reshape(tokens, slice_width)
        gate_add = jnp.dot(block, gate_w[...], preferred_element_type=jnp.float32)
        up_add = jnp.dot(block, up_w[...], preferred_element_type=jnp.float32)

        @pl.when(shard == 0)
        def _():
            gate_acc[...] = gate_add
            up_acc[...] = up_add

        @pl.when(shard != 0)
        def _():
            gate_acc[...] += gate_add
            up_acc[...] += up_add

        @pl.when(shard == shards - 1)
        def _():
            scale = inverse[...]
            gate = gate_acc[...] * scale
            value = gate / (1.0 + jnp.exp(-gate)) * (up_acc[...] * scale) * gates[expert]
            hidden[expert] = value.astype(jnp.bfloat16)

    @pl.when(step >= first_phase)
    def _():
        total = jnp.zeros((tokens, down_w.shape[2]), jnp.float32)
        for e in range(experts_here):
            total += jnp.dot(hidden[e], down_w[e], preferred_element_type=jnp.float32)
        out[...] = total.astype(jnp.bfloat16).reshape(sources, rows, down_w.shape[2])


def run_experts(got, w_gate, w_up, w_down):
    sources, shards, rows, columns = got.shape
    experts_here, width, hidden_local = w_gate.shape
    slice_width = width // shards
    tile = 512 if slice_width % 512 == 0 else 256
    tiles = slice_width // tile
    tokens = sources * rows
    phase = experts_here * shards

    def gate_at(i):
        j = jnp.minimum(i, phase - 1)
        return (lax.div(j, shards), lax.rem(j, shards), 0)

    def down_at(i):
        return (0, 0, jnp.maximum(i - phase, 0))

    def out_at(i):
        n = jnp.maximum(i - phase, 0)
        return (0, lax.div(n, tiles), 0, lax.rem(n, tiles))

    return pl.pallas_call(
        functools.partial(expert_kernel, shards, experts_here, width, slice_width),
        out_shape=jax.ShapeDtypeStruct((sources, shards, rows, slice_width), jnp.bfloat16),
        grid=(phase + shards * tiles,),
        in_specs=[
            pl.BlockSpec((sources, shards, rows, columns), lambda i: (0, 0, 0, 0)),
            pl.BlockSpec((None, slice_width, hidden_local), gate_at),
            pl.BlockSpec((None, slice_width, hidden_local), gate_at),
            pl.BlockSpec((experts_here, hidden_local, tile), down_at),
        ],
        out_specs=pl.BlockSpec((sources, None, rows, tile), out_at),
        scratch_shapes=[
            pltpu.VMEM((tokens, hidden_local), jnp.float32),
            pltpu.VMEM((tokens, hidden_local), jnp.float32),
            pltpu.VMEM((experts_here, tokens, hidden_local), jnp.bfloat16),
            pltpu.VMEM((tokens, 1), jnp.float32),
            pltpu.VMEM((experts_here, tokens, 1), jnp.float32),
        ],
        compiler_params=pltpu.CompilerParams(vmem_limit_bytes=50 * 1024 * 1024),
        cost_estimate=pl.CostEstimate(
            flops=6 * tokens * experts_here * width * hidden_local,
            bytes_accessed=6 * experts_here * width * hidden_local + 4 * tokens * width,
            transcendentals=experts_here * tokens * hidden_local,
        ),
    )(got, w_gate, w_up, w_down)


def in_parts(value):
    high = lax.reduce_precision(value, 8, 7)
    middle = lax.reduce_precision(value - high, 8, 7)
    low = value - high - middle
    return [high, middle, low]


def per_device(
    residual,
    query_new,
    key_new,
    value_new,
    key_cache,
    value_cache,
    lengths,
    norm_gain,
    router,
    routes,
    w_gate,
    w_up,
    w_down,
):
    env_count, step_count, slice_width = residual.shape
    local_experts, width, hidden_local = w_gate.shape
    experts = router.shape[1]
    shards = lax.axis_size("tp")
    sources = lax.axis_size("grp") * lax.axis_size("ex")
    row_count = env_count * step_count
    state = residual.astype(jnp.float32) + attend(
        query_new, key_new, value_new, key_cache, value_cache, lengths
    )
    attended = state.astype(jnp.bfloat16)
    state = state.reshape(row_count, slice_width)
    squares = jnp.sum(state * state, -1)
    scaled = state * norm_gain.astype(jnp.float32)
    logits = jnp.einsum("rd,dx->rx", scaled, router, precision=lax.Precision.HIGHEST)
    pair = routes.reshape(row_count, 2)
    expert_ids = lax.broadcasted_iota(jnp.int32, (1, experts), 1)
    sign = (pair[:, 1:2] == expert_ids).astype(jnp.float32) - (
        pair[:, 0:1] == expert_ids
    ).astype(jnp.float32)
    difference = jnp.sum(sign * logits, -1)
    columns = in_parts(squares) + in_parts(difference)
    columns += [pair[:, 0].astype(jnp.float32), pair[:, 1].astype(jnp.float32)]
    info = jnp.stack(columns, axis=-1)
    info = jnp.pad(info, ((0, 0), (0, LANES - info.shape[1])))
    payload = jnp.concatenate([scaled.astype(jnp.bfloat16), info.astype(jnp.bfloat16)], axis=1)
    got = lax.all_gather(payload, ("grp", "ex", "tp"), axis=0, tiled=True)
    got = got.reshape(sources, shards, row_count, slice_width + LANES)
    terms = run_experts(got, w_gate, w_up, w_down)
    terms = terms.reshape(sources * shards * row_count, slice_width)
    mixed = lax.psum_scatter(terms, ("grp", "ex", "tp"), scatter_dimension=0, tiled=True)
    return (attended, mixed.reshape(env_count, step_count, slice_width))


def solution(mesh):
    return jax.shard_map(
        per_device,
        mesh=mesh,
        in_specs=(
            P(("grp", "ex"), None, "tp"),
            P(("grp", "ex"), None, "tp"),
            P(("grp", "ex"), None, "tp"),
            P(("grp", "ex"), None, "tp"),
            P(("grp", "ex"), "tp", None, None),
            P(("grp", "ex"), "tp", None, None),
            P(("grp", "ex")),
            P("tp"),
            P("tp", None),
            P(("grp", "ex"), None, None),
            P("ex", None, ("grp", "tp")),
            P("ex", None, ("grp", "tp")),
            P("ex", ("grp", "tp"), None),
        ),
        out_specs=(P(("grp", "ex"), None, "tp"), P(("grp", "ex"), None, "tp")),
        check_vma=False,
    )
```

```python
import functools

import jax
import jax.numpy as jnp
from jax import lax
from jax.experimental import pallas as pl
from jax.experimental.pallas import tpu as pltpu
from jax.sharding import PartitionSpec as P

LANES = 128


def attend(query_new, key_new, value_new, key_cache, value_cache, lengths):
    env_count, step_count, feature_count = query_new.shape
    kv_count = key_cache.shape[1]
    context = key_cache.shape[2]
    head_dim = key_cache.shape[3]
    group_size = feature_count // (kv_count * head_dim)
    queries = query_new.reshape(env_count, step_count, kv_count, group_size, head_dim)
    keys_now = key_new.reshape(env_count, step_count, kv_count, head_dim)
    values_now = value_new.reshape(env_count, step_count, kv_count, head_dim)
    score_scale = head_dim ** (-0.5)
    cached = (
        jnp.einsum("eskgd,ekcd->eskgc", queries, key_cache, preferred_element_type=jnp.float32)
        * score_scale
    )
    fresh_scores = (
        jnp.einsum("eskgd,etkd->eskgt", queries, keys_now, preferred_element_type=jnp.float32)
        * score_scale
    )
    valid_mask = (lax.broadcasted_iota(jnp.int32, (env_count, context), 1) < lengths[:, None])[
        :, None, None, None, :
    ]
    causal = (
        lax.broadcasted_iota(jnp.int32, (step_count, step_count), 1)
        <= lax.broadcasted_iota(jnp.int32, (step_count, step_count), 0)
    )[None, :, None, None, :]
    cached = jnp.where(valid_mask, cached, -1e30)
    fresh_scores = jnp.where(causal, fresh_scores, -1e30)
    row_top = jnp.maximum(jnp.max(cached, -1), jnp.max(fresh_scores, -1))[..., None]
    weight_cached = jnp.where(valid_mask, jnp.exp(cached - row_top), 0.0)
    weight_fresh = jnp.where(causal, jnp.exp(fresh_scores - row_top), 0.0)
    row_total = (jnp.sum(weight_cached, -1) + jnp.sum(weight_fresh, -1))[..., None]
    probs_cached = (weight_cached / row_total).astype(jnp.bfloat16)
    probs_fresh = (weight_fresh / row_total).astype(jnp.bfloat16)
    heads_out = jnp.einsum(
        "eskgc,ekcd->eskgd", probs_cached, value_cache, preferred_element_type=jnp.float32
    )
    heads_out = heads_out + jnp.einsum(
        "eskgt,etkd->eskgd", probs_fresh, values_now, preferred_element_type=jnp.float32
    )
    return heads_out.reshape(env_count, step_count, feature_count)


def expert_kernel(
    shards, experts_here, width, slice_width, got, gate_w, up_w, down_w, out, gate_acc, up_acc, hidden, inverse, gates
):
    step = pl.program_id(0)
    sources, _, rows, _ = got.shape
    tokens = sources * rows
    shard = lax.rem(step, shards)
    expert = lax.div(step, shards)
    first_phase = experts_here * shards

    @pl.when(step == 0)
    def _():
        info = jnp.zeros((tokens, LANES), jnp.float32)
        for k in range(shards):
            info += got[:, k, :, slice_width:].astype(jnp.float32).reshape(tokens, LANES)
        routed = got[:, 0, :, slice_width:].astype(jnp.float32).reshape(tokens, LANES)
        squares = info[:, 0:1] + info[:, 1:2] + info[:, 2:3]
        root_mean = jnp.sqrt(squares / width + 1e-05)
        difference = (info[:, 3:4] + info[:, 4:5] + info[:, 5:6]) / root_mean
        first = 1.0 / (1.0 + jnp.exp(difference))
        inverse[...] = 1.0 / root_mean
        base = lax.axis_index("ex") * experts_here
        for e in range(experts_here):
            own = (base + e).astype(jnp.float32)
            gates[e] = jnp.where(routed[:, 6:7] == own, first, 0.0) + jnp.where(
                routed[:, 7:8] == own, 1.0 - first, 0.0
            )

    @pl.when(step < first_phase)
    def _():
        block = got[:, shard, :, :slice_width].reshape(tokens, slice_width)
        gate_add = jnp.dot(block, gate_w[...], preferred_element_type=jnp.float32)
        up_add = jnp.dot(block, up_w[...], preferred_element_type=jnp.float32)

        @pl.when(shard == 0)
        def _():
            gate_acc[...] = gate_add
            up_acc[...] = up_add

        @pl.when(shard != 0)
        def _():
            gate_acc[...] += gate_add
            up_acc[...] += up_add

        @pl.when(shard == shards - 1)
        def _():
            scale = inverse[...]
            gate = gate_acc[...] * scale
            value = gate / (1.0 + jnp.exp(-gate)) * (up_acc[...] * scale) * gates[expert]
            hidden[expert] = value.astype(jnp.bfloat16)

    @pl.when(step >= first_phase)
    def _():
        total = jnp.zeros((tokens, down_w.shape[2]), jnp.float32)
        for e in range(experts_here):
            total += jnp.dot(hidden[e], down_w[e], preferred_element_type=jnp.float32)
        out[...] = total.astype(jnp.bfloat16).reshape(sources, rows, down_w.shape[2])


def run_experts(got, w_gate, w_up, w_down):
    sources, shards, rows, columns = got.shape
    experts_here, width, hidden_local = w_gate.shape
    slice_width = width // shards
    tile = 512 if slice_width % 512 == 0 else 256
    tiles = slice_width // tile
    tokens = sources * rows
    phase = experts_here * shards

    def gate_at(i):
        j = jnp.minimum(i, phase - 1)
        return (lax.div(j, shards), lax.rem(j, shards), 0)

    def down_at(i):
        return (0, 0, jnp.maximum(i - phase, 0))

    def out_at(i):
        n = jnp.maximum(i - phase, 0)
        return (0, lax.div(n, tiles), 0, lax.rem(n, tiles))

    return pl.pallas_call(
        functools.partial(expert_kernel, shards, experts_here, width, slice_width),
        out_shape=jax.ShapeDtypeStruct((sources, shards, rows, slice_width), jnp.bfloat16),
        grid=(phase + shards * tiles,),
        in_specs=[
            pl.BlockSpec((sources, shards, rows, columns), lambda i: (0, 0, 0, 0)),
            pl.BlockSpec((None, slice_width, hidden_local), gate_at),
            pl.BlockSpec((None, slice_width, hidden_local), gate_at),
            pl.BlockSpec((experts_here, hidden_local, tile), down_at),
        ],
        out_specs=pl.BlockSpec((sources, None, rows, tile), out_at),
        scratch_shapes=[
            pltpu.VMEM((tokens, hidden_local), jnp.float32),
            pltpu.VMEM((tokens, hidden_local), jnp.float32),
            pltpu.VMEM((experts_here, tokens, hidden_local), jnp.bfloat16),
            pltpu.VMEM((tokens, 1), jnp.float32),
            pltpu.VMEM((experts_here, tokens, 1), jnp.float32),
        ],
        compiler_params=pltpu.CompilerParams(vmem_limit_bytes=50 * 1024 * 1024),
        cost_estimate=pl.CostEstimate(
            flops=6 * tokens * experts_here * width * hidden_local,
            bytes_accessed=6 * experts_here * width * hidden_local + 4 * tokens * width,
            transcendentals=experts_here * tokens * hidden_local,
        ),
    )(got, w_gate, w_up, w_down)


def in_parts(value):
    high = lax.reduce_precision(value, 8, 7)
    middle = lax.reduce_precision(value - high, 8, 7)
    low = value - high - middle
    return [high, middle, low]


def per_device(
    residual,
    query_new,
    key_new,
    value_new,
    key_cache,
    value_cache,
    lengths,
    norm_gain,
    router,
    routes,
    w_gate,
    w_up,
    w_down,
):
    env_count, step_count, slice_width = residual.shape
    local_experts, width, hidden_local = w_gate.shape
    experts = router.shape[1]
    shards = lax.axis_size("tp")
    groups = lax.axis_size("grp")
    owners = lax.axis_size("ex")
    row_count = env_count * step_count
    state = residual.astype(jnp.float32) + attend(
        query_new, key_new, value_new, key_cache, value_cache, lengths
    )
    attended = state.astype(jnp.bfloat16)
    state = state.reshape(row_count, slice_width)
    squares = jnp.sum(state * state, -1)
    scaled = state * norm_gain.astype(jnp.float32)
    logits = jnp.einsum("rd,dx->rx", scaled, router, precision=lax.Precision.HIGHEST)
    pair = routes.reshape(row_count, 2)
    expert_ids = lax.broadcasted_iota(jnp.int32, (1, experts), 1)
    sign = (pair[:, 1:2] == expert_ids).astype(jnp.float32) - (
        pair[:, 0:1] == expert_ids
    ).astype(jnp.float32)
    difference = jnp.sum(sign * logits, -1)
    columns = in_parts(squares) + in_parts(difference)
    columns += [pair[:, 0].astype(jnp.float32), pair[:, 1].astype(jnp.float32)]
    info = jnp.stack(columns, axis=-1)
    info = jnp.pad(info, ((0, 0), (0, LANES - info.shape[1])))
    payload = jnp.concatenate([scaled.astype(jnp.bfloat16), info.astype(jnp.bfloat16)], axis=1)
    blocks = [payload]
    for r in range(1, owners):
        blocks.append(lax.ppermute(payload, "ex", [(i, (i + r) % owners) for i in range(owners)]))
    got = lax.all_gather(jnp.concatenate(blocks, axis=0), ("grp", "tp"), axis=0, tiled=True)
    got = got.reshape(groups, shards, owners * row_count, slice_width + LANES)
    terms = run_experts(got, w_gate, w_up, w_down)
    terms = terms.reshape(groups * shards * owners * row_count, slice_width)
    summed = lax.psum_scatter(terms, ("grp", "tp"), scatter_dimension=0, tiled=True)
    summed = summed.reshape(owners, row_count, slice_width)
    mixed = summed[0].astype(jnp.float32)
    for r in range(1, owners):
        back = lax.ppermute(summed[r], "ex", [(i, (i - r) % owners) for i in range(owners)])
        mixed = mixed + back.astype(jnp.float32)
    mixed = mixed.astype(jnp.bfloat16)
    return (attended, mixed.reshape(env_count, step_count, slice_width))


def solution(mesh):
    return jax.shard_map(
        per_device,
        mesh=mesh,
        in_specs=(
            P(("grp", "ex"), None, "tp"),
            P(("grp", "ex"), None, "tp"),
            P(("grp", "ex"), None, "tp"),
            P(("grp", "ex"), None, "tp"),
            P(("grp", "ex"), "tp", None, None),
            P(("grp", "ex"), "tp", None, None),
            P(("grp", "ex")),
            P("tp"),
            P("tp", None),
            P(("grp", "ex"), None, None),
            P("ex", None, ("grp", "tp")),
            P("ex", None, ("grp", "tp")),
            P("ex", ("grp", "tp"), None),
        ),
        out_specs=(P(("grp", "ex"), None, "tp"), P(("grp", "ex"), None, "tp")),
        check_vma=False,
    )
```
